512 devices in a mesh: group: 16 (over z_hi, y, core), blk: 32 (over z_lo, x).
Axes of the slice: x: 4, y: 4, z: 16 (z_hi: 2, z_lo: 8; z = z_hi * 8 + z_lo), core: 2. Of those that a mesh axis runs over, the one named last changes fastest.
Arguments:
- images: float32 [131072, 1152], P(('group', 'blk')), may hold values from -0.6 to 0.6
- held_text: float32 [131072, 1152], P(('group', 'blk')), may hold values from -0.6 to 0.6
- log_temp: float32 [1], replicated, may hold values from 1.6 to 2.6
- bias: float32 [1], replicated, may hold values from -4 to -1
Outputs:
- row_loss: float32 [131072], P(('group', 'blk'))
- image_grad: float32 [131072, 1152], P(('group', 'blk'))
- text_grad: float32 [131072, 1152], P(('group', 'blk'))
The draws below stay inside these ranges and needn't reach their ends.
All inputs are finite; a program needn't handle non-finite values.
Results may differ from the reference program's by a relative error of at most 0.0001.
Values sent between devices are 32-bit elements; how exact they have to be, the bound alone decides.
A program may use at most 64 MiB of HBM per device.

```python
import math
import jax
import jax.numpy as jnp
from jax import lax

D = 1152
B_DEV = 256
TOKENS = 131072
N_GROUP = 16
N_BLK = 32


def shard_levels(stream_key, extent, pieces, low, largest):
    gain, own = 1.0, jax.random.fold_in(stream_key, 6)
    for position, shards_of in pieces:
        draws = jnp.exp(jax.random.uniform(jax.random.fold_in(own, position), (shards_of,), jnp.float32, low / len(pieces), largest / len(pieces)))
        gain = gain * jnp.repeat(draws, extent[position] // shards_of).reshape([-1 if axis == position else 1 for axis in range(len(extent))])
    return gain


def normal_values(key, extent, width, most, pieces=(), kind=jnp.bfloat16):
    gain = shard_levels(key, extent, pieces, -0.22, 0.18) if pieces else 1.0
    result = jax.random.normal(key, extent, jnp.float32) * width * gain
    return jnp.minimum(jnp.maximum(result, -most), most).astype(kind)


def setup_inputs(seed: int = 0) -> dict:
    key_list = jax.random.split(jax.random.key(seed), 5)
    images = normal_values(key_list[0], (TOKENS, D), 0.1, 0.6, ((0, 512),), jnp.float32)
    held_text = normal_values(key_list[1], (TOKENS, D), 0.1, 0.6, ((0, 512),), jnp.float32)
    log_temp = jnp.clip(jax.random.uniform(key_list[2], (1,), jnp.float32, 1.6, 2.6), 1.6, 2.6)
    bias = jnp.clip(jax.random.uniform(key_list[3], (1,), jnp.float32, -4.0, -1.0), -4.0, -1.0)
    return dict(images=images, held_text=held_text, log_temp=log_temp, bias=bias)


def pair_blocks(args):
    xblock, yblock, scale, shift = args
    logits = scale * jnp.einsum('kid,kjd->kij', xblock, yblock, precision=lax.Precision.HIGHEST) + shift
    losses = lax.optimization_barrier(jnp.sum(jax.nn.softplus(logits), axis=2))
    weights = jax.nn.sigmoid(logits) / jnp.float32(math.sqrt(4 * B_DEV))
    grad_x = scale * jnp.einsum('kij,kjd->kid', weights, yblock, precision=lax.Precision.HIGHEST)
    grad_y = scale * jnp.einsum('kij,kid->kjd', weights, xblock, precision=lax.Precision.HIGHEST)
    return (losses, grad_x, grad_y)

def reference(images, held_text, log_temp, bias):
    scale = jnp.exp(log_temp[0])
    shift = bias[0]
    xall = images.reshape(N_GROUP, N_BLK, B_DEV, D)
    yall = held_text.reshape(N_GROUP, N_BLK, B_DEV, D)
    losses = jnp.zeros((N_GROUP, N_BLK, B_DEV), jnp.float32)
    grad_x = jnp.zeros((N_GROUP, N_BLK, B_DEV, D), jnp.float32)
    grad_y = jnp.zeros((N_GROUP, N_BLK, B_DEV, D), jnp.float32)
    for offset_g, offset_b in ((0, 0), (0, 1), (1, 2), (1, 3)):
        partner = jnp.roll(yall, (offset_g, offset_b), axis=(0, 1))
        scales = jnp.full((N_GROUP,), scale, jnp.float32)
        shifts = jnp.full((N_GROUP,), shift, jnp.float32)
        part_loss, part_x, part_y = lax.map(pair_blocks, (xall, partner, scales, shifts))
        losses = losses + part_loss
        grad_x = grad_x + part_x
        grad_y = grad_y + jnp.roll(part_y, (-offset_g, -offset_b), axis=(0, 1))
    row_loss = losses.reshape(TOKENS) / jnp.float32(4 * B_DEV)
    return (row_loss, grad_x.reshape(TOKENS, D), grad_y.reshape(TOKENS, D))
```

```python
import functools
import math

import jax
import jax.numpy as jnp
from jax import lax
from jax.experimental import pallas as pl
from jax.experimental.pallas import tpu as pltpu
from jax.sharding import PartitionSpec as P

F32, BF16 = jnp.float32, jnp.bfloat16
MESH = pl.DeviceIdType.MESH
NT = (((1,), (1,)), ((), ()))
NN = (((1,), (0,)), ((), ()))
PARTS = 4


def split(value):
    high = value.astype(BF16)
    return high, (value - high.astype(F32)).astype(BF16)


def dot3(a, b, dims):
    def one(p, q):
        return lax.dot_general(p, q, dims, preferred_element_type=F32)

    return one(a[0], b[0]) + (one(a[0], b[1]) + one(a[1], b[0]))


def device(group, blk):
    return {"group": lax.rem(group + 16, 16), "blk": lax.rem(blk + 32, 32)}


def at(x, y, z, core):
    z_hi, z_lo = z // 8, lax.rem(z, 8)
    return {"group": z_hi * 8 + y * 2 + core, "blk": z_lo * 4 + lax.rem(x + 4, 4)}


def kernel(
    temp_ref, bias_ref, x_hbm, y_hbm, loss_ref, gx_hbm, gy_hbm,
    x_in, y_in, y_far, x_far, xh, xl, yh, yl, wt, gx_own, gy_own, gx_far, gy_far,
    gx_back, gy_back, relay_a, relay_b, loss_part, loss_far, loss_back,
    load_sem, send_sem, recv_sem, out_sem,
):
    rows, width = x_in.shape
    part = rows // PARTS
    group, blk = lax.axis_index("group"), lax.axis_index("blk")
    x, z = lax.rem(blk, 4), (group // 8) * 8 + blk // 4
    y, core = lax.rem(group // 2, 4), lax.rem(group, 2)
    first = lax.rem(group, 8) == 0
    last = lax.rem(group, 8) == 7

    next_blk, prev_blk = device(group, blk + 1), device(group, blk - 1)
    ahead, behind = device(group + 1, blk + 2), device(group - 1, blk - 2)

    def relay_a_at(j):
        return at(x + 2, j, z, 1)

    def relay_b_at(j):
        return at(x, j, z, 0)

    a_from = at(x + 2, 0, z, 0)
    a_to = device(a_from["group"] - 1, a_from["blk"] - 2)
    b_from = at(x, 3, z, 1)
    b_to = device(b_from["group"] + 1, b_from["blk"] + 2)

    def rows_of(j):
        return pl.ds(pl.multiple_of(j * part, part), part)

    def load(k, source, target):
        return pltpu.make_async_copy(source, target, load_sem.at[k])

    load(0, x_hbm, x_in).start()
    load(1, y_hbm, y_in).start()

    barrier = pltpu.get_barrier_semaphore()

    def signal(to):
        pl.semaphore_signal(barrier, inc=1, device_id=to, device_id_type=MESH)

    signal(prev_blk)
    signal(next_blk)

    @pl.when(jnp.logical_not(last))
    def _():
        signal(ahead)

    @pl.when(last)
    def _():
        src = device(group + 1, blk + 2)
        z_src = (src["group"] // 8) * 8 + src["blk"] // 4
        for j in range(PARTS):
            signal(at(lax.rem(src["blk"], 4) + 2, j, z_src, 1))

    @pl.when(jnp.logical_not(first))
    def _():
        signal(behind)

    @pl.when(first)
    def _():
        src = device(group - 1, blk - 2)
        z_src = (src["group"] // 8) * 8 + src["blk"] // 4
        for j in range(PARTS):
            signal(at(lax.rem(src["blk"], 4), j, z_src, 0))
        signal(behind)

    @pl.when(core == 1)
    def _():
        signal(a_from)

    @pl.when(core == 0)
    def _():
        signal(b_from)

    pl.semaphore_wait(barrier, jnp.where(first, PARTS + 4, jnp.where(last, PARTS + 5, 5)))

    def remote(k, source, target, to):
        return pltpu.make_async_remote_copy(
            src_ref=source, dst_ref=target, send_sem=send_sem.at[k], recv_sem=recv_sem.at[k],
            device_id=to, device_id_type=MESH,
        )

    def x_copy(j, to):
        return remote(j, x_hbm.at[rows_of(j)], x_far.at[rows_of(j)], to)

    def x_to_relay(j):
        return pltpu.make_async_remote_copy(
            src_ref=x_hbm.at[rows_of(j)], dst_ref=relay_a, send_sem=send_sem.at[j], recv_sem=recv_sem.at[14],
            device_id=relay_a_at(j), device_id_type=MESH,
        )

    def a_hand_on():
        return pltpu.make_async_remote_copy(
            src_ref=relay_a, dst_ref=x_far.at[rows_of(y)], send_sem=send_sem.at[14], recv_sem=recv_sem.at[y],
            device_id=a_to, device_id_type=MESH,
        )

    def gx_copy(j, to):
        return remote(4 + j, gx_far.at[rows_of(j)], gx_back.at[rows_of(j)], to)

    def gx_to_relay(j):
        return pltpu.make_async_remote_copy(
            src_ref=gx_far.at[rows_of(j)], dst_ref=relay_b, send_sem=send_sem.at[4 + j], recv_sem=recv_sem.at[15],
            device_id=relay_b_at(j), device_id_type=MESH,
        )

    def b_hand_on():
        return pltpu.make_async_remote_copy(
            src_ref=relay_b, dst_ref=gx_back.at[rows_of(y)], send_sem=send_sem.at[15], recv_sem=recv_sem.at[4 + y],
            device_id=b_to, device_id_type=MESH,
        )

    def gy_copy(j):
        return remote(8 + j, gy_far.at[rows_of(j)], gy_back.at[rows_of(j)], prev_blk)

    y_copy = remote(12, y_hbm, y_far, next_blk)
    loss_copy = remote(13, loss_far, loss_back, ahead)

    @pl.when(first)
    def _():
        for j in range(PARTS):
            x_to_relay(j).start()

    y_copy.start()

    @pl.when(jnp.logical_not(first))
    def _():
        for j in range(PARTS):
            x_copy(j, behind).start()

    @pl.when(core == 1)
    def _():
        x_to_relay(0).wait_recv()
        a_hand_on().start()

    scale = jnp.exp(jnp.full((1, rows), temp_ref[0], F32))
    shift = bias_ref[0]
    gain = scale * (1.0 / math.sqrt(4 * rows))

    def pair(products):
        logits = scale * products + shift
        small = jnp.exp(-jnp.abs(logits))
        total = 1.0 + small
        log1p = jnp.where(total == 1.0, small, jnp.log(total) * (small / (total - 1.0)))
        weights = jnp.where(logits >= 0, 1.0, small) / total
        return jnp.maximum(logits, 0.0) + log1p, weights * gain

    def lanes(losses):
        return losses[:, :128] + losses[:, 128:]

    def both(high, low, k, where=slice(None)):
        return high[k, where], low[k, where]

    def split_block(source, k, high, low):
        def step(j, _):
            high[k, rows_of(j)], low[k, rows_of(j)] = split(source[rows_of(j)])
            return 0

        lax.fori_loop(0, PARTS, step, 0)

    load(0, x_hbm, x_in).wait()
    split_block(x_in, 0, xh, xl)
    load(1, y_hbm, y_in).wait()
    split_block(y_in, 0, yh, yl)
    losses, weights = pair(dot3(both(xh, xl, 0), both(yh, yl, 0), NT))
    loss_part[...] = lanes(losses)
    gx_own[...] = dot3(split(weights), both(yh, yl, 0), NN)
    gy_own[...] = dot3(split(weights.T), both(xh, xl, 0), NN)

    y_copy.wait_recv()
    split_block(y_far, 1, yh, yl)
    losses, weights = pair(dot3(both(xh, xl, 0), both(yh, yl, 1), NT))
    loss_part[...] += lanes(losses)
    gx_own[...] += dot3(split(weights), both(yh, yl, 1), NN)
    gy_far[...] = dot3(split(weights.T), both(xh, xl, 0), NN)

    def far_step(j, _):
        x_copy(j, behind).wait_recv()
        here = rows_of(j)
        xh[1, here], xl[1, here] = split(x_far[here])
        image = both(xh, xl, 1, here)
        losses, weights = pair(dot3(image, both(yh, yl, 0), NT))
        loss_far[here] = lanes(losses)
        wt[0, here] = weights
        grad = dot3(split(weights), both(yh, yl, 0), NN)
        losses, weights = pair(dot3(image, both(yh, yl, 1), NT))
        loss_far[here] += lanes(losses)
        wt[1, here] = weights
        gx_far[here] = grad + dot3(split(weights), both(yh, yl, 1), NN)

        @pl.when(last)
        def _():
            gx_to_relay(j).start()

        @pl.when(jnp.logical_not(last))
        def _():
            gx_copy(j, ahead).start()

        return 0

    lax.fori_loop(0, PARTS, far_step, 0)
    loss_copy.start()

    wt[1] = wt[1].T

    def text_step(j, _):
        here = rows_of(j)
        gy_far[here] += dot3(split(wt[1, here]), both(xh, xl, 1), NN)
        gy_copy(j).start()
        return 0

    lax.fori_loop(0, PARTS, text_step, 0)

    @pl.when(core == 0)
    def _():
        gx_to_relay(0).wait_recv()
        b_hand_on().start()

    gy_own[...] += dot3(split(wt[0].T), both(xh, xl, 1), NN)

    def out(k, j, source, target):
        return pltpu.make_async_copy(source.at[rows_of(j)], target.at[rows_of(j)], out_sem.at[4 * k + j])

    for j in range(PARTS):
        gy_copy(j).wait_recv()
        gy_own[rows_of(j)] += gy_back[rows_of(j)]
        out(1, j, gy_own, gy_hbm).start()
    for j in range(PARTS):
        gx_copy(j, ahead).wait_recv()
        gx_own[rows_of(j)] += gx_back[rows_of(j)]
        out(0, j, gx_own, gx_hbm).start()
    loss_copy.wait_recv()
    sums = lax.dot_general(
        jnp.ones((8, 128), F32), loss_part[...] + loss_back[...], NT,
        precision=lax.Precision.HIGHEST, preferred_element_type=F32,
    )
    loss_ref[...] = sums * (1.0 / (4 * rows))

    y_copy.wait_send()
    loss_copy.wait_send()
    for j in range(PARTS):
        x_copy(j, behind).wait_send()
        gx_copy(j, ahead).wait_send()
        gy_copy(j).wait_send()

    @pl.when(core == 1)
    def _():
        a_hand_on().wait_send()

    @pl.when(core == 0)
    def _():
        b_hand_on().wait_send()

    for j in range(PARTS):
        out(1, j, gy_own, gy_hbm).wait()
        out(0, j, gx_own, gx_hbm).wait()


def body(images, held_text, log_temp, bias):
    rows, width = images.shape
    block = pltpu.VMEM((rows, width), F32)
    halves = pltpu.VMEM((2, rows, width), BF16)
    relay = pltpu.VMEM((rows // PARTS, width), F32)
    loss = pltpu.VMEM((rows, 128), F32)
    anywhere = pl.BlockSpec(memory_space=pl.ANY)
    scalar = pl.BlockSpec(memory_space=pltpu.SMEM)
    whole = jax.ShapeDtypeStruct((rows, width), F32)
    row_loss, grad_x, grad_y = pl.pallas_call(
        kernel,
        out_shape=(jax.ShapeDtypeStruct((8, rows), F32), whole, whole),
        in_specs=[scalar, scalar, anywhere, anywhere],
        out_specs=(pl.BlockSpec(memory_space=pltpu.VMEM), anywhere, anywhere),
        scratch_shapes=[
            block, block, block, block, halves, halves, halves, halves,
            pltpu.VMEM((2, rows, rows), F32),
            block, block, block, block, block, block, relay, relay, loss, loss, loss,
            pltpu.SemaphoreType.DMA((2,)),
            pltpu.SemaphoreType.DMA((16,)),
            pltpu.SemaphoreType.DMA((16,)),
            pltpu.SemaphoreType.DMA((8,)),
        ],
        compiler_params=pltpu.CompilerParams(
            collective_id=0, has_side_effects=True, vmem_limit_bytes=48 * 1024 * 1024
        ),
        name="pair_tiles",
    )(log_temp, bias, images, held_text)
    return row_loss[0], grad_x, grad_y


def solution(mesh):
    placed = (P(("group", "blk"), None), P(("group", "blk"), None), P(), P())
    return jax.shard_map(
        body,
        mesh=mesh,
        in_specs=placed,
        out_specs=(P(("group", "blk")), P(("group", "blk"), None), P(("group", "blk"), None)),
        check_vma=False,
    )
```

```python
import math

import jax
import jax.numpy as jnp
from jax import lax
from jax.experimental import pallas as pl
from jax.experimental.pallas import tpu as pltpu
from jax.sharding import PartitionSpec as P

F32, BF16 = jnp.float32, jnp.bfloat16
MESH = pl.DeviceIdType.MESH
NT = (((1,), (1,)), ((), ()))
NN = (((1,), (0,)), ((), ()))
PARTS = 4


def split(value):
    high = value.astype(BF16)
    return high, (value - high.astype(F32)).astype(BF16)


def dot3(a, b, dims):
    def one(p, q):
        return lax.dot_general(p, q, dims, preferred_element_type=F32)

    return one(a[0], b[0]) + (one(a[0], b[1]) + one(a[1], b[0]))


def device(group, blk):
    return {"group": lax.rem(group + 16, 16), "blk": lax.rem(blk + 32, 32)}


def at(x, y, z, core):
    return {"group": (z // 8) * 8 + y * 2 + core, "blk": lax.rem(z, 8) * 4 + x}


def kernel(
    temp_ref, bias_ref, x_hbm, y_hbm, loss_ref, gx_hbm, gy_hbm,
    own, own_high, own_low, far, high, low, grad, relay, loss_part,
    load_sem, send_sem, recv_sem, out_sem,
):
    rows = own.shape[1]
    part = rows // PARTS
    group, blk = lax.axis_index("group"), lax.axis_index("blk")
    x, z = lax.rem(blk, 4), (group // 8) * 8 + blk // 4
    y, core = lax.rem(group // 2, 4), lax.rem(group, 2)
    first = lax.rem(group, 8) == 0
    last = lax.rem(group, 8) == 7
    edge = first | last
    near = jnp.where(first, 1, 0)
    late = 1 - near
    relays = (x == 1) | (x == 2)

    def step(kind):
        return 1 - 2 * kind

    def along(kind):
        return device(group, blk + step(kind))

    def across(kind):
        return device(group + step(kind), blk + step(kind))

    def ring(x_from):
        return jnp.where(x_from >= 2, 2, 1)

    def relay_of(kind, holder, j):
        z_from = (holder["group"] // 8) * 8 + holder["blk"] // 4
        return at(ring(lax.rem(holder["blk"], 4)), j, z_from, kind)

    def served(slot):
        z_hi, z_lo = z // 8, lax.rem(z, 8)
        return device(z_hi * 8 + jnp.where(core == 0, 7, 0), z_lo * 4 + 2 * (x - 1) + slot)

    def rows_of(j):
        return pl.ds(pl.multiple_of(j * part, part), part)

    load_x = pltpu.make_async_copy(x_hbm, own.at[1], load_sem.at[1])
    load_y = pltpu.make_async_copy(y_hbm, own.at[0], load_sem.at[0])
    load_y.start()
    load_x.start()

    barrier = pltpu.get_barrier_semaphore()

    def signal(to):
        pl.semaphore_signal(barrier, inc=1, device_id=to, device_id_type=MESH)

    signal(along(0))
    signal(along(1))

    @pl.when(jnp.logical_not(first))
    def _():
        signal(across(1))

    @pl.when(jnp.logical_not(last))
    def _():
        signal(across(0))

    @pl.when(edge)
    def _():
        holder = device(group - step(late), blk - 2 * step(late))
        for j in range(PARTS):
            signal(relay_of(late, holder, j))

    @pl.when(relays)
    def _():
        signal(served(0))
        signal(served(1))

    pl.semaphore_wait(barrier, jnp.where(edge, PARTS + 3, 4) + jnp.where(relays, 2, 0))
    load_y.wait()
    load_x.wait()

    def copy(kind, leg, j, source, to):
        k = kind * 12 + leg * 4 + j
        return pltpu.make_async_remote_copy(
            src_ref=source, dst_ref=far.at[kind, leg, rows_of(j)], send_sem=send_sem.at[k], recv_sem=recv_sem.at[k],
            device_id=to, device_id_type=MESH,
        )

    def leg0(kind, j):
        return copy(kind, 0, j, own.at[kind, rows_of(j)], along(kind))

    def leg1(kind, j):
        return copy(kind, 1, j, far.at[kind, 0, rows_of(j)], across(kind))

    def leg2(kind, j):
        return copy(kind, 2, j, far.at[kind, 1, rows_of(j)], along(kind))

    def to_relay(j):
        me = {"group": group, "blk": blk}
        return pltpu.make_async_remote_copy(
            src_ref=own.at[near, rows_of(j)], dst_ref=relay.at[lax.rem(x, 2)],
            send_sem=send_sem.at[near * 12 + 4 + j], recv_sem=recv_sem.at[24 + lax.rem(x, 2)],
            device_id=relay_of(near, me, j), device_id_type=MESH,
        )

    def from_relay(slot):
        holder = served(slot)
        return pltpu.make_async_remote_copy(
            src_ref=relay.at[slot], dst_ref=far.at[core, 1, rows_of(y)],
            send_sem=send_sem.at[24 + slot], recv_sem=recv_sem.at[core * 12 + 4 + y],
            device_id=device(holder["group"] + step(core), holder["blk"] + 2 * step(core)), device_id_type=MESH,
        )

    def relay_in(slot):
        return pltpu.make_async_remote_copy(
            src_ref=own.at[0, rows_of(0)], dst_ref=relay.at[slot],
            send_sem=send_sem.at[24 + slot], recv_sem=recv_sem.at[24 + slot],
            device_id=along(0), device_id_type=MESH,
        )

    @pl.when(edge)
    def _():
        for j in range(PARTS):
            to_relay(j).start()

    for j in range(2):
        for kind in range(2):
            leg0(kind, j).start()

    scale = jnp.exp(jnp.full((1, rows), temp_ref[0], F32))
    shift = bias_ref[0]
    gain = scale * (1.0 / math.sqrt(4 * rows))

    def pair(products):
        logits = scale * products + shift
        small = jnp.exp(-jnp.abs(logits))
        total = 1.0 + small
        log1p = jnp.where(total == 1.0, small, jnp.log(total) * (small / (total - 1.0)))
        weights = jnp.where(logits >= 0, 1.0, small) / total
        losses = jnp.maximum(logits, 0.0) + log1p
        return losses[:, :128] + losses[:, 128:], weights * gain

    def held(kind):
        return own_high[kind], own_low[kind]

    def own_part(j, _):
        here = rows_of(j)
        for kind in range(2):
            own_high[kind, here], own_low[kind, here] = split(own[kind, here])
        return 0

    lax.fori_loop(0, PARTS, own_part, 0)

    losses, weights = pair(dot3(held(1), held(0), NT))
    loss_part[0] = losses
    grad[0] = dot3(split(weights), held(0), NN)
    grad[1] = dot3(split(weights.T), held(1), NN)

    def meet(kind, leg):
        def part_of(j, _):
            here = rows_of(j)
            high[here], low[here] = split(far[kind, leg, here])
            return 0

        lax.fori_loop(0, PARTS, part_of, 0)
        other = (high[...], low[...])
        mine = 1 - kind
        losses, weights = pair(dot3((own_high[mine], own_low[mine]), other, NT))
        loss_part[kind] += losses
        grad[kind] += dot3(split(weights), other, NN)

    loss_part[1] = jnp.zeros_like(loss_part[1])

    def take0(j):
        for kind in range(2):
            leg0(kind, j).wait_recv()

            @pl.when(jnp.logical_not(edge & (near == kind)))
            def _():
                leg1(kind, j).start()

            leg0(kind, j).wait_send()
            if j + 2 < PARTS:
                leg0(kind, j + 2).start()

    def take1(kind, j):
        leg1(kind, j).wait_recv()
        leg2(kind, j).start()

    def take1_ordinary(j):
        @pl.when(edge)
        def _():
            take1(near, j)

        @pl.when(jnp.logical_not(edge))
        def _():
            take1(0, j)
            take1(1, j)

    take0(0)
    take0(1)

    @pl.when(relays)
    def _():
        for slot in range(2):
            relay_in(slot).wait_recv()
            from_relay(slot).start()

    take1_ordinary(0)
    take0(2)
    take1_ordinary(1)
    take0(3)
    meet(0, 0)
    take1_ordinary(2)
    meet(1, 0)
    take1_ordinary(3)
    meet(near, 1)

    @pl.when(edge)
    def _():
        for j in range(PARTS):
            take1(late, j)

    meet(late, 1)
    for j in range(PARTS):
        leg2(near, j).wait_recv()
    meet(near, 2)

    write_x = pltpu.make_async_copy(grad.at[0], gx_hbm, out_sem.at[0])
    write_y = pltpu.make_async_copy(grad.at[1], gy_hbm, out_sem.at[1])

    @pl.when(first)
    def _():
        write_y.start()

    @pl.when(jnp.logical_not(first))
    def _():
        write_x.start()

    for j in range(PARTS):
        leg2(late, j).wait_recv()
    meet(late, 2)

    @pl.when(first)
    def _():
        write_x.start()

    @pl.when(jnp.logical_not(first))
    def _():
        write_y.start()

    loss_ref[...] = lax.dot_general(
        jnp.ones((8, 128), F32), loss_part[0], NT, precision=lax.Precision.HIGHEST, preferred_element_type=F32
    ) * (1.0 / (4 * rows))

    for kind in range(2):
        for j in range(PARTS):
            leg1(kind, j).wait_send()
            leg2(kind, j).wait_send()

    @pl.when(relays)
    def _():
        from_relay(0).wait_send()
        from_relay(1).wait_send()

    write_x.wait()
    write_y.wait()


def body(images, held_text, log_temp, bias):
    rows, width = images.shape
    pieces = pltpu.VMEM((2, rows, width), F32)
    halves = pltpu.VMEM((2, rows, width), BF16)
    half = pltpu.VMEM((rows, width), BF16)
    in_hbm = pl.BlockSpec(memory_space=pltpu.HBM)
    scalar = pl.BlockSpec(memory_space=pltpu.SMEM)
    whole = jax.ShapeDtypeStruct((rows, width), F32)
    row_loss, grad_x, grad_y = pl.pallas_call(
        kernel,
        out_shape=(jax.ShapeDtypeStruct((8, rows), F32), whole, whole),
        in_specs=[scalar, scalar, in_hbm, in_hbm],
        out_specs=(pl.BlockSpec(memory_space=pltpu.VMEM), in_hbm, in_hbm),
        scratch_shapes=[
            pieces, halves, halves,
            pltpu.VMEM((2, 3, rows, width), F32),
            half, half, pieces,
            pltpu.VMEM((2, rows // PARTS, width), F32),
            pltpu.VMEM((2, rows, 128), F32),
            pltpu.SemaphoreType.DMA((2,)),
            pltpu.SemaphoreType.DMA((26,)),
            pltpu.SemaphoreType.DMA((26,)),
            pltpu.SemaphoreType.DMA((2,)),
        ],
        compiler_params=pltpu.CompilerParams(
            collective_id=0, has_side_effects=True, vmem_limit_bytes=60 * 1024 * 1024
        ),
        name="pair_tiles",
    )(log_temp, bias, images, held_text)
    return row_loss[0], grad_x, grad_y


def solution(mesh):
    placed = (P(("group", "blk"), None), P(("group", "blk"), None), P(), P())
    return jax.shard_map(
        body,
        mesh=mesh,
        in_specs=placed,
        out_specs=(P(("group", "blk")), P(("group", "blk"), None), P(("group", "blk"), None)),
        check_vma=False,
    )
```

```python
import math

import jax
import jax.numpy as jnp
from jax import lax
from jax.experimental import pallas as pl
from jax.experimental.pallas import tpu as pltpu
from jax.sharding import PartitionSpec as P

F32, BF16 = jnp.float32, jnp.bfloat16
MESH = pl.DeviceIdType.MESH
NT = (((1,), (1,)), ((), ()))
NN = (((1,), (0,)), ((), ()))
PARTS = 4


def split(value):
    high = value.astype(BF16)
    return high, (value - high.astype(F32)).astype(BF16)


def dot3(a, b, dims):
    def one(p, q):
        return lax.dot_general(p, q, dims, preferred_element_type=F32)

    return one(a[0], b[0]) + (one(a[0], b[1]) + one(a[1], b[0]))


def device(group, blk):
    return {"group": lax.rem(group + 16, 16), "blk": lax.rem(blk + 32, 32)}


def at(x, y, z, core):
    return {"group": (z // 8) * 8 + y * 2 + core, "blk": lax.rem(z, 8) * 4 + x}


def kernel(
    temp_ref, bias_ref, x_hbm, y_hbm, loss_ref, gx_hbm, gy_hbm,
    own, own_high, own_low, far, high, low, grad, relay, loss_part,
    load_sem, send_sem, recv_sem, out_sem,
):
    rows = own.shape[1]
    part = rows // PARTS
    group, blk = lax.axis_index("group"), lax.axis_index("blk")
    x, z = lax.rem(blk, 4), (group // 8) * 8 + blk // 4
    y, core = lax.rem(group // 2, 4), lax.rem(group, 2)
    first = lax.rem(group, 8) == 0
    last = lax.rem(group, 8) == 7
    edge = first | last
    near = jnp.where(first, 1, 0)
    late = 1 - near
    inner = (x == 1) | (x == 2)
    outer = jnp.logical_not(inner)

    def step(kind):
        return 1 - 2 * kind

    def along(kind):
        return device(group, blk + step(kind))

    def across(kind):
        return device(group + step(kind), blk + step(kind))

    def ring(x_from):
        return jnp.where(x_from == 0, 2, jnp.where(x_from == 3, 1, x_from))

    def relay_of(kind, holder, j):
        z_from = (holder["group"] // 8) * 8 + holder["blk"] // 4
        return at(ring(lax.rem(holder["blk"], 4)), j, z_from, kind)

    def served(slot):
        x_from = x if slot == 0 else jnp.where(x == 2, 0, 3)
        return at(x_from, jnp.where(core == 0, 3, 0), z, 1 - core)

    pass_to, pass_from = at(ring(x), y, z, core), at(jnp.where(x == 2, 0, 3), y, z, core)

    def rows_of(j):
        return pl.ds(pl.multiple_of(j * part, part), part)

    load_x = pltpu.make_async_copy(x_hbm, own.at[1], load_sem.at[1])
    load_y = pltpu.make_async_copy(y_hbm, own.at[0], load_sem.at[0])
    load_y.start()
    load_x.start()

    barrier = pltpu.get_barrier_semaphore()

    def signal(to):
        pl.semaphore_signal(barrier, inc=1, device_id=to, device_id_type=MESH)

    signal(along(0))
    signal(along(1))

    @pl.when(jnp.logical_not(first))
    def _():
        signal(across(1))

    @pl.when(jnp.logical_not(last))
    def _():
        signal(across(0))

    @pl.when(edge)
    def _():
        holder = device(group - step(late), blk - 2 * step(late))
        for j in range(PARTS):
            signal(relay_of(late, holder, j))

    signal(served(0))

    @pl.when(inner)
    def _():
        signal(pass_from)

    pl.semaphore_wait(barrier, jnp.where(edge, PARTS + 3, 4) + jnp.where(inner, 2, 1))
    load_y.wait()
    load_x.wait()

    def copy(kind, leg, j, source, to):
        k = kind * 12 + leg * 4 + j
        return pltpu.make_async_remote_copy(
            src_ref=source, dst_ref=far.at[kind, leg, rows_of(j)], send_sem=send_sem.at[k], recv_sem=recv_sem.at[k],
            device_id=to, device_id_type=MESH,
        )

    def leg0(kind, j):
        return copy(kind, 0, j, own.at[kind, rows_of(j)], along(kind))

    def leg1(kind, j):
        return copy(kind, 1, j, far.at[kind, 0, rows_of(j)], across(kind))

    def leg2(kind, j):
        return copy(kind, 2, j, far.at[kind, 1, rows_of(j)], along(kind))

    def hop(source, target, k_send, k_recv, to):
        return pltpu.make_async_remote_copy(
            src_ref=source, dst_ref=target, send_sem=send_sem.at[k_send], recv_sem=recv_sem.at[k_recv],
            device_id=to, device_id_type=MESH,
        )

    def to_relay(j):
        return hop(own.at[near, rows_of(j)], relay.at[0], near * 12 + 4 + j, 24, at(x, j, z, near))

    def pass_on():
        return hop(relay.at[0], relay.at[1], 24, 25, pass_to)

    def from_relay(slot):
        holder = served(slot)
        to = device(holder["group"] + step(core), holder["blk"] + 2 * step(core))
        return hop(relay.at[slot], far.at[core, 1, rows_of(y)], 24 + slot, core * 12 + 4 + y, to)

    @pl.when(edge)
    def _():
        for j in range(PARTS):
            to_relay(j).start()

    for j in range(2):
        for kind in range(2):
            leg0(kind, j).start()

    scale = jnp.exp(jnp.full((1, rows), temp_ref[0], F32))
    shift = bias_ref[0]

    def pair(products):
        logits = scale[:, : products.shape[1]] * products + shift
        small = jnp.exp(-jnp.abs(logits))
        total = 1.0 + small
        log1p = jnp.where(total == 1.0, small, jnp.log(total) * (small / (total - 1.0)))
        weights = jnp.where(logits >= 0, 1.0, small) / total
        return jnp.maximum(logits, 0.0) + log1p, weights

    def held(kind):
        return own_high[kind], own_low[kind]

    def own_part(j, _):
        here = rows_of(j)
        for kind in range(2):
            own_high[kind, here], own_low[kind, here] = split(own[kind, here])
        return 0

    lax.fori_loop(0, PARTS, own_part, 0)

    losses, weights = pair(dot3(held(1), held(0), NT))
    loss_part[0] = losses[:, :128] + losses[:, 128:]
    grad[0] = dot3(split(weights), held(0), NN)
    grad[1] = dot3(split(weights.T), held(1), NN)

    def meet_half(kind, leg, half):
        lines = rows // 2
        other = split(far[kind, leg, half * lines : (half + 1) * lines])
        mine = 1 - kind
        losses, weights = pair(dot3((own_high[mine], own_low[mine]), other, NT))
        loss_part[kind] += losses
        grad[kind] += dot3(split(weights), other, NN)

    def meet(kind, leg):
        def part_of(j, _):
            here = rows_of(j)
            high[here], low[here] = split(far[kind, leg, here])
            return 0

        lax.fori_loop(0, PARTS, part_of, 0)
        other = (high[...], low[...])
        mine = 1 - kind
        losses, weights = pair(dot3((own_high[mine], own_low[mine]), other, NT))
        loss_part[kind] += losses[:, :128] + losses[:, 128:]
        grad[kind] += dot3(split(weights), other, NN)

    loss_part[1] = jnp.zeros_like(loss_part[1])

    def take0(j):
        for kind in range(2):
            leg0(kind, j).wait_recv()

            @pl.when(jnp.logical_not(edge & (near == kind)))
            def _():
                leg1(kind, j).start()

            leg0(kind, j).wait_send()
            if j + 2 < PARTS:
                leg0(kind, j + 2).start()

    def take1(kind, j):
        leg1(kind, j).wait_recv()
        leg2(kind, j).start()

    def take1_ordinary(j):
        @pl.when(edge)
        def _():
            take1(near, j)

        @pl.when(jnp.logical_not(edge))
        def _():
            take1(0, j)
            take1(1, j)

    hop(relay.at[0], relay.at[0], 24, 24, along(0)).wait_recv()

    @pl.when(inner)
    def _():
        from_relay(0).start()

    @pl.when(outer)
    def _():
        pass_on().start()

    take0(0)
    take0(1)

    @pl.when(inner)
    def _():
        hop(relay.at[1], relay.at[1], 25, 25, along(0)).wait_recv()
        from_relay(1).start()

    take1_ordinary(0)
    take0(2)
    take1_ordinary(1)
    take0(3)
    meet(0, 0)
    take1_ordinary(2)
    meet(1, 0)
    take1_ordinary(3)
    meet(near, 1)

    @pl.when(edge)
    def _():
        for j in range(PARTS):
            take1(late, j)

    meet(late, 1)
    for half in range(2):
        for kind in (near, late):
            for j in range(half * PARTS // 2, (half + 1) * PARTS // 2):
                leg2(kind, j).wait_recv()
            meet_half(kind, 2, half)

    write_x = pltpu.make_async_copy(grad.at[0], gx_hbm, out_sem.at[0])
    write_y = pltpu.make_async_copy(grad.at[1], gy_hbm, out_sem.at[1])
    write_x.start()
    write_y.start()

    loss_ref[...] = lax.dot_general(
        jnp.ones((8, 128), F32), loss_part[0], NT, precision=lax.Precision.HIGHEST, preferred_element_type=F32
    )

    for kind in range(2):
        for j in range(PARTS):
            leg1(kind, j).wait_send()
            leg2(kind, j).wait_send()

    from_relay(0).wait_send()

    @pl.when(inner)
    def _():
        from_relay(1).wait_send()

    write_x.wait()
    write_y.wait()


def body(images, held_text, log_temp, bias):
    rows, width = images.shape
    pieces = pltpu.VMEM((2, rows, width), F32)
    halves = pltpu.VMEM((2, rows, width), BF16)
    half = pltpu.VMEM((rows, width), BF16)
    in_hbm = pl.BlockSpec(memory_space=pltpu.HBM)
    scalar = pl.BlockSpec(memory_space=pltpu.SMEM)
    whole = jax.ShapeDtypeStruct((rows, width), F32)
    losses, grad_x, grad_y = pl.pallas_call(
        kernel,
        out_shape=(jax.ShapeDtypeStruct((8, rows), F32), whole, whole),
        in_specs=[scalar, scalar, in_hbm, in_hbm],
        out_specs=(pl.BlockSpec(memory_space=pltpu.VMEM), in_hbm, in_hbm),
        scratch_shapes=[
            pieces, halves, halves,
            pltpu.VMEM((2, 3, rows, width), F32),
            half, half, pieces,
            pltpu.VMEM((2, rows // PARTS, width), F32),
            pltpu.VMEM((2, rows, 128), F32),
            pltpu.SemaphoreType.DMA((2,)),
            pltpu.SemaphoreType.DMA((26,)),
            pltpu.SemaphoreType.DMA((26,)),
            pltpu.SemaphoreType.DMA((2,)),
        ],
        compiler_params=pltpu.CompilerParams(
            collective_id=0, has_side_effects=True, vmem_limit_bytes=60 * 1024 * 1024
        ),
        name="pair_tiles",
    )(log_temp, bias, images, held_text)
    gain = jnp.exp(log_temp) * (1.0 / math.sqrt(4 * rows))
    return losses[0] * (1.0 / (4 * rows)), grad_x * gain, grad_y * gain


def solution(mesh):
    placed = (P(("group", "blk"), None), P(("group", "blk"), None), P(), P())
    return jax.shard_map(
        body,
        mesh=mesh,
        in_specs=placed,
        out_specs=(P(("group", "blk")), P(("group", "blk"), None), P(("group", "blk"), None)),
        check_vma=False,
    )
```

```python
import math

import jax
import jax.numpy as jnp
from jax import lax
from jax.experimental import pallas as pl
from jax.experimental.pallas import tpu as pltpu
from jax.sharding import PartitionSpec as P

F32, BF16 = jnp.float32, jnp.bfloat16
MESH = pl.DeviceIdType.MESH
NT = (((1,), (1,)), ((), ()))
NN = (((1,), (0,)), ((), ()))
PARTS = 4


def split(value):
    high = value.astype(BF16)
    return high, (value - high.astype(F32)).astype(BF16)


def dot3(a, b, dims):
    def one(p, q):
        return lax.dot_general(p, q, dims, preferred_element_type=F32)

    return one(a[0], b[0]) + (one(a[0], b[1]) + one(a[1], b[0]))


def device(group, blk):
    return {"group": lax.rem(group + 16, 16), "blk": lax.rem(blk + 32, 32)}


def at(x, y, z, core):
    return {"group": (z // 8) * 8 + y * 2 + core, "blk": lax.rem(z, 8) * 4 + x}


def kernel(
    temp_ref, bias_ref, x_hbm, y_hbm, loss_ref, gx_hbm, gy_hbm,
    own, own_high, own_low, far, high, low, grad, relay, loss_part,
    load_sem, send_sem, recv_sem, out_sem, go_sem,
):
    rows = own.shape[1]
    part = rows // PARTS
    group, blk = lax.axis_index("group"), lax.axis_index("blk")
    x, z = lax.rem(blk, 4), (group // 8) * 8 + blk // 4
    y, core = lax.rem(group // 2, 4), lax.rem(group, 2)
    first = lax.rem(group, 8) == 0
    last = lax.rem(group, 8) == 7
    edge = first | last
    near = jnp.where(first, 1, 0)
    late = 1 - near
    inner = (x == 1) | (x == 2)
    outer = jnp.logical_not(inner)

    low_z = z < 8
    blk_start, blk_end = low_z & (blk == 0), low_z & (blk == 31)

    def step(kind):
        return 1 - 2 * kind

    def along(kind):
        return device(group, blk + step(kind))

    def across(kind):
        return device(group + step(kind), blk + step(kind))

    def ring(x_from):
        return jnp.where(x_from == 0, 2, jnp.where(x_from == 3, 1, x_from))

    def relay_of(kind, holder, j):
        z_from = (holder["group"] // 8) * 8 + holder["blk"] // 4
        return at(ring(lax.rem(holder["blk"], 4)), j, z_from, kind)

    def served(slot):
        x_from = x if slot == 0 else jnp.where(x == 2, 0, 3)
        return at(x_from, jnp.where(core == 0, 3, 0), z, 1 - core)

    pass_to, pass_from = at(ring(x), y, z, core), at(jnp.where(x == 2, 0, 3), y, z, core)

    def rows_of(j):
        return pl.ds(pl.multiple_of(j * part, part), part)

    load_x = pltpu.make_async_copy(x_hbm, own.at[1], load_sem.at[1])
    load_y = pltpu.make_async_copy(y_hbm, own.at[0], load_sem.at[0])
    load_y.start()
    load_x.start()

    barrier = pltpu.get_barrier_semaphore()

    def signal(to):
        pl.semaphore_signal(barrier, inc=1, device_id=to, device_id_type=MESH)

    def receiver(slot):
        holder = served(slot)
        return device(holder["group"] + step(core), holder["blk"] + 2 * step(core))

    signal(along(1))

    @pl.when(jnp.logical_not(first))
    def _():
        signal(across(1))

    @pl.when(jnp.logical_not(blk_end))
    def _():
        signal(along(0))

    @pl.when(jnp.logical_not(blk_end | last))
    def _():
        signal(across(0))

    def each_late_relay(use):
        holder = device(group - step(late), blk - 2 * step(late))
        for j in range(PARTS):
            use(relay_of(late, holder, j), holder)

    @pl.when(edge & low_z)
    def _():
        each_late_relay(lambda to, holder: signal(to))

    signal(served(0))

    @pl.when(inner)
    def _():
        signal(pass_from)

    @pl.when(inner & low_z)
    def _():
        signal(receiver(0))
        signal(receiver(1))

    senders = jnp.where(edge, PARTS + 3, 4) - jnp.where(blk_start, jnp.where(first, 1, 2), 0)
    passing = jnp.where(inner, jnp.where(low_z, 0, 2), 1)
    pl.semaphore_wait(barrier, senders + passing + jnp.where(edge & jnp.logical_not(low_z), PARTS, 0))

    def go(k, to):
        pl.semaphore_signal(go_sem.at[k], inc=1, device_id=to, device_id_type=MESH)

    @pl.when(edge & jnp.logical_not(low_z))
    def _():
        def tell(to, holder):
            x_from = lax.rem(holder["blk"], 4)
            go(jnp.where((x_from == 0) | (x_from == 3), 1, 0), to)

        each_late_relay(tell)

    @pl.when(blk_end)
    def _():
        go(2, along(0))

    @pl.when(blk_end & jnp.logical_not(last))
    def _():
        go(3, across(0))

    load_y.wait()
    load_x.wait()

    def copy(kind, leg, j, source, to):
        k = kind * 12 + leg * 4 + j
        return pltpu.make_async_remote_copy(
            src_ref=source, dst_ref=far.at[kind, leg, rows_of(j)], send_sem=send_sem.at[k], recv_sem=recv_sem.at[k],
            device_id=to, device_id_type=MESH,
        )

    def leg0(kind, j):
        return copy(kind, 0, j, own.at[kind, rows_of(j)], along(kind))

    def leg1(kind, j):
        return copy(kind, 1, j, far.at[kind, 0, rows_of(j)], across(kind))

    def leg2(kind, j):
        return copy(kind, 2, j, far.at[kind, 1, rows_of(j)], along(kind))

    def hop(source, target, k_send, k_recv, to):
        return pltpu.make_async_remote_copy(
            src_ref=source, dst_ref=target, send_sem=send_sem.at[k_send], recv_sem=recv_sem.at[k_recv],
            device_id=to, device_id_type=MESH,
        )

    def to_relay(j):
        return hop(own.at[near, rows_of(j)], relay.at[0], near * 12 + 4 + j, 24, at(x, j, z, near))

    def pass_on():
        return hop(relay.at[0], relay.at[1], 24, 25, pass_to)

    def from_relay(slot):
        return hop(relay.at[slot], far.at[core, 1, rows_of(y)], 24 + slot, core * 12 + 4 + y, receiver(slot))

    @pl.when(edge)
    def _():
        for j in range(PARTS):
            to_relay(j).start()

    leg0(0, 0).start()

    @pl.when(jnp.logical_not(blk_start))
    def _():
        leg0(1, 0).start()
        leg0(1, 1).start()

    leg0(0, 1).start()

    scale = jnp.exp(jnp.full((1, rows), temp_ref[0], F32))
    shift = bias_ref[0]

    def pair(products):
        logits = scale[:, : products.shape[1]] * products + shift
        small = jnp.exp(-jnp.abs(logits))
        total = 1.0 + small
        log1p = jnp.where(total == 1.0, small, jnp.log(total) * (small / (total - 1.0)))
        weights = jnp.where(logits >= 0, 1.0, small) / total
        return jnp.maximum(logits, 0.0) + log1p, weights

    def held(kind):
        return own_high[kind], own_low[kind]

    def own_part(j, _):
        here = rows_of(j)
        for kind in range(2):
            own_high[kind, here], own_low[kind, here] = split(own[kind, here])
        return 0

    lax.fori_loop(0, PARTS, own_part, 0)

    losses, weights = pair(dot3(held(1), held(0), NT))
    loss_part[0] = losses[:, :128] + losses[:, 128:]
    grad[0] = dot3(split(weights), held(0), NN)
    grad[1] = dot3(split(weights.T), held(1), NN)

    def meet_half(kind, leg, half):
        lines = rows // 2
        other = split(far[kind, leg, half * lines : (half + 1) * lines])
        mine = 1 - kind
        losses, weights = pair(dot3((own_high[mine], own_low[mine]), other, NT))
        loss_part[kind] += losses
        grad[kind] += dot3(split(weights), other, NN)

    def meet(kind, leg):
        def part_of(j, _):
            here = rows_of(j)
            high[here], low[here] = split(far[kind, leg, here])
            return 0

        lax.fori_loop(0, PARTS, part_of, 0)
        other = (high[...], low[...])
        mine = 1 - kind
        losses, weights = pair(dot3((own_high[mine], own_low[mine]), other, NT))
        loss_part[kind] += losses[:, :128] + losses[:, 128:]
        grad[kind] += dot3(split(weights), other, NN)

    loss_part[1] = jnp.zeros_like(loss_part[1])

    def take0(j):
        for kind in range(2):
            leg0(kind, j).wait_recv()

            @pl.when(jnp.logical_not(edge & (near == kind)))
            def _():
                leg1(kind, j).start()

            leg0(kind, j).wait_send()
            if j + 2 < PARTS:
                leg0(kind, j + 2).start()

    def take1(kind, j):
        leg1(kind, j).wait_recv()
        leg2(kind, j).start()

    def take1_ordinary(j):
        @pl.when(edge)
        def _():
            take1(near, j)

        @pl.when(jnp.logical_not(edge))
        def _():
            take1(0, j)
            take1(1, j)

    @pl.when(blk_start)
    def _():
        pl.semaphore_wait(go_sem.at[2], 1)
        leg0(1, 0).start()
        leg0(1, 1).start()

    @pl.when(blk_start & jnp.logical_not(first))
    def _():
        pl.semaphore_wait(go_sem.at[3], 1)

    hop(relay.at[0], relay.at[0], 24, 24, along(0)).wait_recv()

    @pl.when(outer)
    def _():
        pass_on().start()

    @pl.when(inner & jnp.logical_not(low_z))
    def _():
        from_relay(0).start()

    take0(0)

    @pl.when(inner & low_z)
    def _():
        pl.semaphore_wait(go_sem.at[0], 1)
        from_relay(0).start()

    take0(1)

    @pl.when(inner & low_z)
    def _():
        pl.semaphore_wait(go_sem.at[1], 1)

    @pl.when(inner)
    def _():
        hop(relay.at[1], relay.at[1], 25, 25, along(0)).wait_recv()
        from_relay(1).start()

    take1_ordinary(0)
    take0(2)
    take1_ordinary(1)
    take0(3)
    meet(0, 0)
    take1_ordinary(2)
    meet(1, 0)
    take1_ordinary(3)
    meet(near, 1)

    @pl.when(edge)
    def _():
        for j in range(PARTS):
            take1(late, j)

    meet(late, 1)
    write_x = pltpu.make_async_copy(grad.at[0], gx_hbm, out_sem.at[0])
    write_y = pltpu.make_async_copy(grad.at[1], gy_hbm, out_sem.at[1])

    def last_half(kind, half):
        for j in range(half * PARTS // 2, (half + 1) * PARTS // 2):
            leg2(kind, j).wait_recv()
        meet_half(kind, 2, half)

    last_half(near, 0)
    last_half(late, 0)
    last_half(near, 1)

    @pl.when(first)
    def _():
        write_y.start()

    @pl.when(jnp.logical_not(first))
    def _():
        write_x.start()

    last_half(late, 1)

    @pl.when(first)
    def _():
        write_x.start()

    @pl.when(jnp.logical_not(first))
    def _():
        write_y.start()

    loss_ref[...] = lax.dot_general(
        jnp.ones((8, 128), F32), loss_part[0], NT, precision=lax.Precision.HIGHEST, preferred_element_type=F32
    )

    for kind in range(2):
        for j in range(PARTS):
            leg1(kind, j).wait_send()
            leg2(kind, j).wait_send()

    from_relay(0).wait_send()

    @pl.when(inner)
    def _():
        from_relay(1).wait_send()

    write_x.wait()
    write_y.wait()


def body(images, held_text, log_temp, bias):
    rows, width = images.shape
    pieces = pltpu.VMEM((2, rows, width), F32)
    halves = pltpu.VMEM((2, rows, width), BF16)
    half = pltpu.VMEM((rows, width), BF16)
    in_hbm = pl.BlockSpec(memory_space=pltpu.HBM)
    scalar = pl.BlockSpec(memory_space=pltpu.SMEM)
    whole = jax.ShapeDtypeStruct((rows, width), F32)
    losses, grad_x, grad_y = pl.pallas_call(
        kernel,
        out_shape=(jax.ShapeDtypeStruct((8, rows), F32), whole, whole),
        in_specs=[scalar, scalar, in_hbm, in_hbm],
        out_specs=(pl.BlockSpec(memory_space=pltpu.VMEM), in_hbm, in_hbm),
        scratch_shapes=[
            pieces, halves, halves,
            pltpu.VMEM((2, 3, rows, width), F32),
            half, half, pieces,
            pltpu.VMEM((2, rows // PARTS, width), F32),
            pltpu.VMEM((2, rows, 128), F32),
            pltpu.SemaphoreType.DMA((2,)),
            pltpu.SemaphoreType.DMA((26,)),
            pltpu.SemaphoreType.DMA((26,)),
            pltpu.SemaphoreType.DMA((2,)),
            pltpu.SemaphoreType.REGULAR((4,)),
        ],
        compiler_params=pltpu.CompilerParams(
            collective_id=0, has_side_effects=True, vmem_limit_bytes=51 * 1024 * 1024
        ),
        name="pair_tiles",
    )(log_temp, bias, images, held_text)
    gain = jnp.exp(log_temp) * (1.0 / math.sqrt(4 * rows))
    return losses[0] * (1.0 / (4 * rows)), grad_x * gain, grad_y * gain


def solution(mesh):
    placed = (P(("group", "blk"), None), P(("group", "blk"), None), P(), P())
    return jax.shard_map(
        body,
        mesh=mesh,
        in_specs=placed,
        out_specs=(P(("group", "blk")), P(("group", "blk"), None), P(("group", "blk"), None)),
        check_vma=False,
    )
```

```python
import math

import jax
import jax.numpy as jnp
from jax import lax
from jax.experimental import pallas as pl
from jax.experimental.pallas import tpu as pltpu
from jax.sharding import PartitionSpec as P

F32, BF16 = jnp.float32, jnp.bfloat16
MESH = pl.DeviceIdType.MESH
NT = (((1,), (1,)), ((), ()))
NN = (((1,), (0,)), ((), ()))
PARTS = 4


def split(value):
    high = value.astype(BF16)
    return high, (value - high.astype(F32)).astype(BF16)


def dot3(a, b, dims):
    def one(p, q):
        return lax.dot_general(p, q, dims, preferred_element_type=F32)

    return one(a[0], b[0]) + (one(a[0], b[1]) + one(a[1], b[0]))


def device(group, blk):
    return {"group": lax.rem(group + 16, 16), "blk": lax.rem(blk + 32, 32)}


def at(x, y, z, core):
    return {"group": (z // 8) * 8 + y * 2 + core, "blk": lax.rem(z, 8) * 4 + x}


def kernel(
    temp_ref, bias_ref, x_hbm, y_hbm, loss_ref, gx_hbm, gy_hbm,
    own, own_high, own_low, far, high, low, grad, relay, loss_part,
    load_sem, send_sem, recv_sem, out_sem, go_sem,
):
    rows = own.shape[1]
    part = rows // PARTS
    group, blk = lax.axis_index("group"), lax.axis_index("blk")
    x, z = lax.rem(blk, 4), (group // 8) * 8 + blk // 4
    y, core = lax.rem(group // 2, 4), lax.rem(group, 2)
    first = lax.rem(group, 8) == 0
    last = lax.rem(group, 8) == 7
    edge = first | last
    near = jnp.where(first, 1, 0)
    late = 1 - near
    inner = (x == 1) | (x == 2)
    outer = jnp.logical_not(inner)
    hub = x == jnp.where(core == 0, 2, 1)

    low_z = z < 8
    blk_start, blk_end = low_z & (blk == 0), low_z & (blk == 31)

    def step(kind):
        return 1 - 2 * kind

    def along(kind):
        return device(group, blk + step(kind))

    def across(kind):
        return device(group + step(kind), blk + step(kind))

    def ring(x_from, kind):
        return jnp.where((x_from == 0) | (x_from == 3), jnp.where(kind == 0, 2, 1), x_from)

    def slot_of(x_from):
        return jnp.where(x_from == 0, 1, jnp.where(x_from == 3, 2, 0))

    def relay_of(kind, holder, j):
        z_from = (holder["group"] // 8) * 8 + holder["blk"] // 4
        return at(ring(lax.rem(holder["blk"], 4), kind), j, z_from, kind)

    def served(slot):
        return at((x, 0, 3)[slot], jnp.where(core == 0, 3, 0), z, 1 - core)

    pass_to = at(ring(x, core), y, z, core)

    def rows_of(j):
        return pl.ds(pl.multiple_of(j * part, part), part)

    load_x = pltpu.make_async_copy(x_hbm, own.at[1], load_sem.at[1])
    load_y = pltpu.make_async_copy(y_hbm, own.at[0], load_sem.at[0])
    load_y.start()
    load_x.start()

    barrier = pltpu.get_barrier_semaphore()

    def signal(to):
        pl.semaphore_signal(barrier, inc=1, device_id=to, device_id_type=MESH)

    def receiver(slot):
        holder = served(slot)
        return device(holder["group"] + step(core), holder["blk"] + 3 * step(core))

    signal(along(1))

    @pl.when(jnp.logical_not(first))
    def _():
        signal(across(1))

    @pl.when(jnp.logical_not(blk_end))
    def _():
        signal(along(0))

    @pl.when(jnp.logical_not(blk_end | last))
    def _():
        signal(across(0))

    def each_late_relay(use):
        holder = device(group - step(late), blk - 3 * step(late))
        for j in range(PARTS):
            use(relay_of(late, holder, j), holder)

    @pl.when(edge & low_z)
    def _():
        each_late_relay(lambda to, holder: signal(to))

    signal(served(0))

    @pl.when(hub)
    def _():
        signal(at(0, y, z, core))
        signal(at(3, y, z, core))

    @pl.when(inner & low_z)
    def _():
        signal(receiver(0))

    @pl.when(hub & low_z)
    def _():
        signal(receiver(1))
        signal(receiver(2))

    senders = jnp.where(edge, PARTS + 3, 4) - jnp.where(blk_start, jnp.where(first, 1, 2), 0)
    passing = jnp.where(outer, 1, jnp.where(low_z, 0, jnp.where(hub, 3, 1)))
    pl.semaphore_wait(barrier, senders + passing + jnp.where(edge & jnp.logical_not(low_z), PARTS, 0))

    def go(k, to):
        pl.semaphore_signal(go_sem.at[k], inc=1, device_id=to, device_id_type=MESH)

    @pl.when(edge & jnp.logical_not(low_z))
    def _():
        def tell(to, holder):
            go(slot_of(lax.rem(holder["blk"], 4)), to)

        each_late_relay(tell)

    @pl.when(blk_end)
    def _():
        go(3, along(0))

    @pl.when(blk_end & jnp.logical_not(last))
    def _():
        go(4, across(0))

    load_y.wait()
    load_x.wait()

    def copy(kind, leg, j, source, to):
        k = kind * 12 + leg * 4 + j
        return pltpu.make_async_remote_copy(
            src_ref=source, dst_ref=far.at[kind, leg, rows_of(j)], send_sem=send_sem.at[k], recv_sem=recv_sem.at[k],
            device_id=to, device_id_type=MESH,
        )

    def leg0(kind, j):
        return copy(kind, 0, j, own.at[kind, rows_of(j)], along(kind))

    def leg1(kind, j):
        return copy(kind, 1, j, far.at[kind, 0, rows_of(j)], across(kind))

    def leg2(kind, j):
        back = edge & (late == kind)
        return copy(kind, 2, j, far.at[kind, 1, rows_of(j)], device(group, blk + jnp.where(back, -step(kind), step(kind))))

    def hop(source, target, k_send, k_recv, to):
        return pltpu.make_async_remote_copy(
            src_ref=source, dst_ref=target, send_sem=send_sem.at[k_send], recv_sem=recv_sem.at[k_recv],
            device_id=to, device_id_type=MESH,
        )

    def to_relay(j):
        return hop(own.at[near, rows_of(j)], relay.at[0], near * 12 + 4 + j, 24, at(x, j, z, near))

    def pass_on():
        return hop(relay.at[0], relay.at[slot_of(x)], 24, 24 + slot_of(x), pass_to)

    def from_relay(slot):
        return hop(relay.at[slot], far.at[core, 1, rows_of(y)], 24 + slot, core * 12 + 4 + y, receiver(slot))

    @pl.when(edge)
    def _():
        for j in range(PARTS):
            to_relay(j).start()

    leg0(0, 0).start()

    @pl.when(jnp.logical_not(blk_start))
    def _():
        leg0(1, 0).start()
        leg0(1, 1).start()

    leg0(0, 1).start()

    scale = jnp.exp(jnp.full((1, rows), temp_ref[0], F32))
    shift = bias_ref[0]

    def pair(products):
        logits = scale[:, : products.shape[1]] * products + shift
        small = jnp.exp(-jnp.abs(logits))
        total = 1.0 + small
        log1p = jnp.where(total == 1.0, small, jnp.log(total) * (small / (total - 1.0)))
        weights = jnp.where(logits >= 0, 1.0, small) / total
        return jnp.maximum(logits, 0.0) + log1p, weights

    def held(kind):
        return own_high[kind], own_low[kind]

    def own_part(j, _):
        here = rows_of(j)
        for kind in range(2):
            own_high[kind, here], own_low[kind, here] = split(own[kind, here])
        return 0

    lax.fori_loop(0, PARTS, own_part, 0)

    losses, weights = pair(dot3(held(1), held(0), NT))
    loss_part[0] = losses[:, :128] + losses[:, 128:]
    grad[0] = dot3(split(weights), held(0), NN)
    grad[1] = dot3(split(weights.T), held(1), NN)

    def meet_half(kind, leg, half):
        lines = rows // 2
        other = split(far[kind, leg, half * lines : (half + 1) * lines])
        mine = 1 - kind
        losses, weights = pair(dot3((own_high[mine], own_low[mine]), other, NT))
        loss_part[kind] += losses
        grad[kind] += dot3(split(weights), other, NN)

    def meet(kind, leg):
        def part_of(j, _):
            here = rows_of(j)
            high[here], low[here] = split(far[kind, leg, here])
            return 0

        lax.fori_loop(0, PARTS, part_of, 0)
        other = (high[...], low[...])
        mine = 1 - kind
        losses, weights = pair(dot3((own_high[mine], own_low[mine]), other, NT))
        loss_part[kind] += losses[:, :128] + losses[:, 128:]
        grad[kind] += dot3(split(weights), other, NN)

    loss_part[1] = jnp.zeros_like(loss_part[1])

    def take0(j):
        for kind in range(2):
            leg0(kind, j).wait_recv()

            @pl.when(jnp.logical_not(edge & (near == kind)))
            def _():
                leg1(kind, j).start()

            leg0(kind, j).wait_send()
            if j + 2 < PARTS:
                leg0(kind, j + 2).start()

    def take1(kind, j):
        leg1(kind, j).wait_recv()
        leg2(kind, j).start()

    def take1_ordinary(j):
        @pl.when(edge)
        def _():
            take1(near, j)

        @pl.when(jnp.logical_not(edge))
        def _():
            take1(0, j)
            take1(1, j)

    @pl.when(blk_start)
    def _():
        pl.semaphore_wait(go_sem.at[3], 1)
        leg0(1, 0).start()
        leg0(1, 1).start()

    @pl.when(blk_start & jnp.logical_not(first))
    def _():
        pl.semaphore_wait(go_sem.at[4], 1)

    hop(relay.at[0], relay.at[0], 24, 24, along(0)).wait_recv()

    @pl.when(outer)
    def _():
        pass_on().start()

    @pl.when(inner & jnp.logical_not(low_z))
    def _():
        from_relay(0).start()

    take0(0)

    @pl.when(inner & low_z)
    def _():
        pl.semaphore_wait(go_sem.at[0], 1)
        from_relay(0).start()

    take0(1)

    for slot in (1, 2):
        @pl.when(hub & low_z)
        def _():
            pl.semaphore_wait(go_sem.at[slot], 1)

        @pl.when(hub)
        def _():
            hop(relay.at[slot], relay.at[slot], 24 + slot, 24 + slot, along(0)).wait_recv()
            from_relay(slot).start()

    take1_ordinary(0)
    take0(2)
    take1_ordinary(1)
    take0(3)
    meet(0, 0)
    take1_ordinary(2)
    meet(1, 0)
    take1_ordinary(3)
    meet(near, 1)

    @pl.when(edge)
    def _():
        for j in range(PARTS):
            take1(late, j)

    meet(late, 1)
    write_x = pltpu.make_async_copy(grad.at[0], gx_hbm, out_sem.at[0])
    write_y = pltpu.make_async_copy(grad.at[1], gy_hbm, out_sem.at[1])

    def last_half(kind, half):
        for j in range(half * PARTS // 2, (half + 1) * PARTS // 2):
            leg2(kind, j).wait_recv()
        meet_half(kind, 2, half)

    last_half(near, 0)
    last_half(late, 0)
    last_half(near, 1)

    @pl.when(first)
    def _():
        write_y.start()

    @pl.when(jnp.logical_not(first))
    def _():
        write_x.start()

    last_half(late, 1)

    @pl.when(first)
    def _():
        write_x.start()

    @pl.when(jnp.logical_not(first))
    def _():
        write_y.start()

    loss_ref[...] = lax.dot_general(
        jnp.ones((8, 128), F32), loss_part[0], NT, precision=lax.Precision.HIGHEST, preferred_element_type=F32
    )

    for kind in range(2):
        for j in range(PARTS):
            leg1(kind, j).wait_send()
            leg2(kind, j).wait_send()

    from_relay(0).wait_send()

    @pl.when(hub)
    def _():
        from_relay(1).wait_send()
        from_relay(2).wait_send()

    write_x.wait()
    write_y.wait()


def body(images, held_text, log_temp, bias):
    rows, width = images.shape
    pieces = pltpu.VMEM((2, rows, width), F32)
    halves = pltpu.VMEM((2, rows, width), BF16)
    half = pltpu.VMEM((rows, width), BF16)
    in_hbm = pl.BlockSpec(memory_space=pltpu.HBM)
    scalar = pl.BlockSpec(memory_space=pltpu.SMEM)
    whole = jax.ShapeDtypeStruct((rows, width), F32)
    losses, grad_x, grad_y = pl.pallas_call(
        kernel,
        out_shape=(jax.ShapeDtypeStruct((8, rows), F32), whole, whole),
        in_specs=[scalar, scalar, in_hbm, in_hbm],
        out_specs=(pl.BlockSpec(memory_space=pltpu.VMEM), in_hbm, in_hbm),
        scratch_shapes=[
            pieces, halves, halves,
            pltpu.VMEM((2, 3, rows, width), F32),
            half, half, pieces,
            pltpu.VMEM((3, rows // PARTS, width), F32),
            pltpu.VMEM((2, rows, 128), F32),
            pltpu.SemaphoreType.DMA((2,)),
            pltpu.SemaphoreType.DMA((27,)),
            pltpu.SemaphoreType.DMA((27,)),
            pltpu.SemaphoreType.DMA((2,)),
            pltpu.SemaphoreType.REGULAR((5,)),
        ],
        compiler_params=pltpu.CompilerParams(
            collective_id=0, has_side_effects=True, vmem_limit_bytes=51 * 1024 * 1024
        ),
        name="pair_tiles",
    )(log_temp, bias, images, held_text)
    gain = jnp.exp(log_temp) * (1.0 / math.sqrt(4 * rows))
    return losses[0] * (1.0 / (4 * rows)), grad_x * gain, grad_y * gain


def solution(mesh):
    placed = (P(("group", "blk"), None), P(("group", "blk"), None), P(), P())
    return jax.shard_map(
        body,
        mesh=mesh,
        in_specs=placed,
        out_specs=(P(("group", "blk")), P(("group", "blk"), None), P(("group", "blk"), None)),
        check_vma=False,
    )
```

```python
import math

import jax
import jax.numpy as jnp
from jax import lax
from jax.experimental import pallas as pl
from jax.experimental.pallas import tpu as pltpu
from jax.sharding import PartitionSpec as P

F32, BF16 = jnp.float32, jnp.bfloat16
MESH = pl.DeviceIdType.MESH
NT = (((1,), (1,)), ((), ()))
NN = (((1,), (0,)), ((), ()))
PARTS = 4


def split(value):
    high = value.astype(BF16)
    return high, (value - high.astype(F32)).astype(BF16)


def dot3(a, b, dims):
    def one(p, q):
        return lax.dot_general(p, q, dims, preferred_element_type=F32)

    if dims == NN:
        return one(jnp.concatenate([a[0], a[0], a[1]], axis=1), jnp.concatenate([b[0], b[1], b[0]], axis=0))
    return one(a[0], b[0]) + (one(a[0], b[1]) + one(a[1], b[0]))


def device(group, blk):
    return {"group": lax.rem(group + 16, 16), "blk": lax.rem(blk + 32, 32)}


def at(x, y, z, core):
    return {"group": (z // 8) * 8 + y * 2 + core, "blk": lax.rem(z, 8) * 4 + x}


def kernel(
    temp_ref, bias_ref, x_hbm, y_hbm, loss_ref, gx_hbm, gy_hbm,
    own, own_high, own_low, far, high, low, grad, relay, loss_part,
    load_sem, send_sem, recv_sem, out_sem, go_sem,
):
    rows = own.shape[1]
    part = rows // PARTS
    group, blk = lax.axis_index("group"), lax.axis_index("blk")
    x, z = lax.rem(blk, 4), (group // 8) * 8 + blk // 4
    y, core = lax.rem(group // 2, 4), lax.rem(group, 2)
    first = lax.rem(group, 8) == 0
    last = lax.rem(group, 8) == 7
    edge = first | last
    near = jnp.where(first | ((blk == 0) & jnp.logical_not(last)), 1, 0)
    late = 1 - near
    inner = (x == 1) | (x == 2)
    outer = jnp.logical_not(inner)
    hub = x == jnp.where(core == 0, 2, 1)

    low_z = z < 8
    blk_start, blk_end = low_z & (blk == 0), low_z & (blk == 31)

    def step(kind):
        return 1 - 2 * kind

    def along(kind):
        return device(group, blk + step(kind))

    def across(kind):
        return device(group + step(kind), blk + step(kind))

    def ring(x_from, kind):
        return jnp.where((x_from == 0) | (x_from == 3), jnp.where(kind == 0, 2, 1), x_from)

    def slot_of(x_from):
        return jnp.where(x_from == 0, 1, jnp.where(x_from == 3, 2, 0))

    def relay_of(kind, holder, j):
        z_from = (holder["group"] // 8) * 8 + holder["blk"] // 4
        return at(ring(lax.rem(holder["blk"], 4), kind), j, z_from, kind)

    def served(slot):
        return at((x, 0, 3)[slot], jnp.where(core == 0, 3, 0), z, 1 - core)

    pass_to = at(ring(x, core), y, z, core)

    def rows_of(j):
        return pl.ds(pl.multiple_of(j * part, part), part)

    load_x = pltpu.make_async_copy(x_hbm, own.at[1], load_sem.at[1])
    load_y = pltpu.make_async_copy(y_hbm, own.at[0], load_sem.at[0])
    load_y.start()
    load_x.start()

    barrier = pltpu.get_barrier_semaphore()

    def signal(to):
        pl.semaphore_signal(barrier, inc=1, device_id=to, device_id_type=MESH)

    def receiver(slot):
        holder = served(slot)
        return device(holder["group"] + step(core), holder["blk"] + 3 * step(core))

    signal(along(1))

    @pl.when(jnp.logical_not(first))
    def _():
        signal(across(1))

    @pl.when(jnp.logical_not(blk_end))
    def _():
        signal(along(0))

    @pl.when(jnp.logical_not(blk_end | last))
    def _():
        signal(across(0))

    def each_late_relay(use):
        holder = device(group - step(late), blk - 3 * step(late))
        for j in range(PARTS):
            use(relay_of(late, holder, j), holder)

    @pl.when(edge & low_z)
    def _():
        each_late_relay(lambda to, holder: signal(to))

    signal(served(0))

    @pl.when(hub)
    def _():
        signal(at(0, y, z, core))
        signal(at(3, y, z, core))

    @pl.when(inner & low_z)
    def _():
        signal(receiver(0))

    @pl.when(hub & low_z)
    def _():
        signal(receiver(1))
        signal(receiver(2))

    senders = jnp.where(edge, PARTS + 3, 4) - jnp.where(blk_start, jnp.where(first, 1, 2), 0)
    passing = jnp.where(outer, 1, jnp.where(low_z, 0, jnp.where(hub, 3, 1)))
    pl.semaphore_wait(barrier, senders + passing + jnp.where(edge & jnp.logical_not(low_z), PARTS, 0))

    def go(k, to):
        pl.semaphore_signal(go_sem.at[k], inc=1, device_id=to, device_id_type=MESH)

    @pl.when(edge & jnp.logical_not(low_z))
    def _():
        def tell(to, holder):
            go(slot_of(lax.rem(holder["blk"], 4)), to)

        each_late_relay(tell)

    @pl.when(blk_end)
    def _():
        go(3, along(0))

    @pl.when(blk_end & jnp.logical_not(last))
    def _():
        go(4, across(0))

    load_y.wait()
    load_x.wait()

    def copy(kind, leg, j, source, to):
        k = kind * 12 + leg * 4 + j
        return pltpu.make_async_remote_copy(
            src_ref=source, dst_ref=far.at[kind, leg, rows_of(j)], send_sem=send_sem.at[k], recv_sem=recv_sem.at[k],
            device_id=to, device_id_type=MESH,
        )

    def leg0(kind, j):
        return copy(kind, 0, j, own.at[kind, rows_of(j)], along(kind))

    def leg1(kind, j):
        return copy(kind, 1, j, far.at[kind, 0, rows_of(j)], across(kind))

    def leg2(kind, j):
        back = edge & (late == kind)
        return copy(kind, 2, j, far.at[kind, 1, rows_of(j)], device(group, blk + jnp.where(back, -step(kind), step(kind))))

    def hop(source, target, k_send, k_recv, to):
        return pltpu.make_async_remote_copy(
            src_ref=source, dst_ref=target, send_sem=send_sem.at[k_send], recv_sem=recv_sem.at[k_recv],
            device_id=to, device_id_type=MESH,
        )

    def to_relay(j):
        return hop(own.at[near, rows_of(j)], relay.at[0], near * 12 + 4 + j, 24, at(x, j, z, near))

    def pass_on():
        return hop(relay.at[0], relay.at[slot_of(x)], 24, 24 + slot_of(x), pass_to)

    def from_relay(slot):
        return hop(relay.at[slot], far.at[core, 1, rows_of(y)], 24 + slot, core * 12 + 4 + y, receiver(slot))

    @pl.when(edge)
    def _():
        for j in range(PARTS):
            to_relay(j).start()

    leg0(0, 0).start()

    @pl.when(jnp.logical_not(blk_start))
    def _():
        leg0(1, 0).start()
        leg0(1, 1).start()

    leg0(0, 1).start()

    scale = jnp.exp(jnp.full((1, rows), temp_ref[0], F32))
    shift = bias_ref[0]

    def pair(products):
        logits = scale[:, : products.shape[1]] * products + shift
        small = jnp.exp(-jnp.abs(logits))
        total = 1.0 + small
        log1p = jnp.where(total == 1.0, small, jnp.log(total) * (small / (total - 1.0)))
        weights = jnp.where(logits >= 0, 1.0, small) / total
        return jnp.maximum(logits, 0.0) + log1p, weights * scale[:, : products.shape[1]]

    def held(kind):
        return own_high[kind], own_low[kind]

    def own_part(j, _):
        here = rows_of(j)
        for kind in range(2):
            own_high[kind, here], own_low[kind, here] = split(own[kind, here])
        return 0

    lax.fori_loop(0, PARTS, own_part, 0)

    losses, weights = pair(dot3(held(1), held(0), NT))
    loss_part[0] = losses[:, :128] + losses[:, 128:]
    grad[0] = dot3(split(weights), held(0), NN)
    grad[1] = dot3(split(weights.T), held(1), NN)

    def meet_half(kind, leg, half):
        lines = rows // 2
        other = split(far[kind, leg, half * lines : (half + 1) * lines])
        mine = 1 - kind
        losses, weights = pair(dot3((own_high[mine], own_low[mine]), other, NT))
        loss_part[kind] += losses
        grad[kind] += dot3(split(weights), other, NN)

    def meet(kind, leg):
        def part_of(j, _):
            here = rows_of(j)
            high[here], low[here] = split(far[kind, leg, here])
            return 0

        lax.fori_loop(0, PARTS, part_of, 0)
        other = (high[...], low[...])
        mine = 1 - kind
        losses, weights = pair(dot3((own_high[mine], own_low[mine]), other, NT))
        loss_part[kind] += losses[:, :128] + losses[:, 128:]
        grad[kind] += dot3(split(weights), other, NN)

    loss_part[1] = jnp.zeros_like(loss_part[1])

    def take0(j):
        for kind in range(2):
            leg0(kind, j).wait_recv()

            @pl.when(jnp.logical_not(edge & (near == kind)))
            def _():
                leg1(kind, j).start()

            leg0(kind, j).wait_send()
            if j + 2 < PARTS:
                leg0(kind, j + 2).start()

    def take1(kind, j):
        leg1(kind, j).wait_recv()
        leg2(kind, j).start()

    def take1_ordinary(j):
        @pl.when(edge)
        def _():
            take1(near, j)

        @pl.when(jnp.logical_not(edge))
        def _():
            take1(0, j)
            take1(1, j)

    @pl.when(blk_start)
    def _():
        pl.semaphore_wait(go_sem.at[3], 1)
        leg0(1, 0).start()
        leg0(1, 1).start()

    @pl.when(blk_start & jnp.logical_not(first))
    def _():
        pl.semaphore_wait(go_sem.at[4], 1)

    hop(relay.at[0], relay.at[0], 24, 24, along(0)).wait_recv()

    @pl.when(outer)
    def _():
        pass_on().start()

    @pl.when(inner & jnp.logical_not(low_z))
    def _():
        from_relay(0).start()

    take0(0)

    @pl.when(inner & low_z)
    def _():
        pl.semaphore_wait(go_sem.at[0], 1)
        from_relay(0).start()

    for slot in (1, 2):
        @pl.when(hub & low_z)
        def _():
            pl.semaphore_wait(go_sem.at[slot], 1)

        @pl.when(hub)
        def _():
            hop(relay.at[slot], relay.at[slot], 24 + slot, 24 + slot, along(0)).wait_recv()
            from_relay(slot).start()

    take0(1)

    take1_ordinary(0)
    take0(2)
    take1_ordinary(1)
    take0(3)
    meet(0, 0)
    take1_ordinary(2)
    meet(1, 0)
    take1_ordinary(3)
    meet(near, 1)

    @pl.when(edge)
    def _():
        for j in range(PARTS):
            take1(late, j)

    meet(late, 1)
    write_x = pltpu.make_async_copy(grad.at[0], gx_hbm, out_sem.at[0])
    write_y = pltpu.make_async_copy(grad.at[1], gy_hbm, out_sem.at[1])

    def last_half(kind, half):
        for j in range(half * PARTS // 2, (half + 1) * PARTS // 2):
            leg2(kind, j).wait_recv()
        meet_half(kind, 2, half)

    sooner = jnp.where(blk == 0, 1, near)
    last_half(sooner, 0)
    last_half(1 - sooner, 0)
    last_half(sooner, 1)

    @pl.when(sooner == 1)
    def _():
        write_y.start()

    @pl.when(sooner == 0)
    def _():
        write_x.start()

    last_half(1 - sooner, 1)

    @pl.when(sooner == 1)
    def _():
        write_x.start()

    @pl.when(sooner == 0)
    def _():
        write_y.start()

    loss_ref[...] = lax.dot_general(
        jnp.ones((8, 128), F32), loss_part[0], NT, precision=lax.Precision.HIGHEST, preferred_element_type=F32
    )

    for kind in range(2):
        for j in range(PARTS):
            leg1(kind, j).wait_send()
            leg2(kind, j).wait_send()

    from_relay(0).wait_send()

    @pl.when(hub)
    def _():
        from_relay(1).wait_send()
        from_relay(2).wait_send()

    write_x.wait()
    write_y.wait()


def body(images, held_text, log_temp, bias):
    rows, width = images.shape
    pieces = pltpu.VMEM((2, rows, width), F32)
    halves = pltpu.VMEM((2, rows, width), BF16)
    half = pltpu.VMEM((rows, width), BF16)
    in_hbm = pl.BlockSpec(memory_space=pltpu.HBM)
    scalar = pl.BlockSpec(memory_space=pltpu.SMEM)
    whole = jax.ShapeDtypeStruct((rows, width), F32)
    losses, grad_x, grad_y = pl.pallas_call(
        kernel,
        out_shape=(jax.ShapeDtypeStruct((8, rows), F32), whole, whole),
        in_specs=[scalar, scalar, in_hbm, in_hbm],
        out_specs=(pl.BlockSpec(memory_space=pltpu.VMEM), in_hbm, in_hbm),
        scratch_shapes=[
            pieces, halves, halves,
            pltpu.VMEM((2, 3, rows, width), F32),
            half, half, pieces,
            pltpu.VMEM((3, rows // PARTS, width), F32),
            pltpu.VMEM((2, rows, 128), F32),
            pltpu.SemaphoreType.DMA((2,)),
            pltpu.SemaphoreType.DMA((27,)),
            pltpu.SemaphoreType.DMA((27,)),
            pltpu.SemaphoreType.DMA((2,)),
            pltpu.SemaphoreType.REGULAR((5,)),
        ],
        compiler_params=pltpu.CompilerParams(
            collective_id=0, has_side_effects=True, vmem_limit_bytes=51 * 1024 * 1024
        ),
        name="pair_tiles",
    )(log_temp, bias, images, held_text)
    gain = 1.0 / math.sqrt(4 * rows)
    return losses[0] * (1.0 / (4 * rows)), grad_x * gain, grad_y * gain


def solution(mesh):
    placed = (P(("group", "blk"), None), P(("group", "blk"), None), P(), P())
    return jax.shard_map(
        body,
        mesh=mesh,
        in_specs=placed,
        out_specs=(P(("group", "blk")), P(("group", "blk"), None), P(("group", "blk"), None)),
        check_vma=False,
    )
```

```python
import math

import jax
import jax.numpy as jnp
from jax import lax
from jax.experimental import pallas as pl
from jax.experimental.pallas import tpu as pltpu
from jax.sharding import PartitionSpec as P

F32, BF16 = jnp.float32, jnp.bfloat16
MESH = pl.DeviceIdType.MESH
NT = (((1,), (1,)), ((), ()))
NN = (((1,), (0,)), ((), ()))
PARTS = 4


def split(value):
    high = value.astype(BF16)
    return high, (value - high.astype(F32)).astype(BF16)


def dot3(a, b, dims):
    def one(p, q):
        return lax.dot_general(p, q, dims, preferred_element_type=F32)

    if dims == NN:
        return one(jnp.concatenate([a[0], a[0], a[1]], axis=1), jnp.concatenate([b[0], b[1], b[0]], axis=0))
    return one(a[0], b[0]) + (one(a[0], b[1]) + one(a[1], b[0]))


def device(group, blk):
    return {"group": lax.rem(group + 16, 16), "blk": lax.rem(blk + 32, 32)}


def at(x, y, z, core):
    return {"group": (z // 8) * 8 + y * 2 + core, "blk": lax.rem(z, 8) * 4 + x}


def kernel(
    temp_ref, bias_ref, x_hbm, y_hbm, loss_ref, gx_hbm, gy_hbm,
    own, own_high, own_low, far, high, low, grad, relay, loss_part,
    load_sem, send_sem, recv_sem, out_sem, go_sem,
):
    rows = own.shape[1]
    part = rows // PARTS
    group, blk = lax.axis_index("group"), lax.axis_index("blk")
    x, z = lax.rem(blk, 4), (group // 8) * 8 + blk // 4
    y, core = lax.rem(group // 2, 4), lax.rem(group, 2)
    first = lax.rem(group, 8) == 0
    last = lax.rem(group, 8) == 7
    edge = first | last
    near = jnp.where(first | ((blk == 0) & jnp.logical_not(last)), 1, 0)
    late = 1 - near
    inner = (x == 1) | (x == 2)
    outer = jnp.logical_not(inner)
    hub = x == jnp.where(core == 0, 2, 1)

    low_z = z < 8
    blk_start, blk_end = low_z & (blk == 0), low_z & (blk == 31)

    def step(kind):
        return 1 - 2 * kind

    def along(kind):
        return device(group, blk + step(kind))

    def across(kind):
        return device(group + step(kind), blk + step(kind))

    def ring(x_from, kind):
        return jnp.where((x_from == 0) | (x_from == 3), jnp.where(kind == 0, 2, 1), x_from)

    def slot_of(x_from):
        return jnp.where(x_from == 0, 1, jnp.where(x_from == 3, 2, 0))

    def relay_of(kind, holder, j):
        z_from = (holder["group"] // 8) * 8 + holder["blk"] // 4
        return at(ring(lax.rem(holder["blk"], 4), kind), j, z_from, kind)

    def served(slot):
        return at((x, 0, 3)[slot], jnp.where(core == 0, 3, 0), z, 1 - core)

    pass_to = at(ring(x, core), y, z, core)

    def rows_of(j):
        return pl.ds(pl.multiple_of(j * part, part), part)

    load_x = pltpu.make_async_copy(x_hbm, own.at[1], load_sem.at[1])
    load_y = pltpu.make_async_copy(y_hbm, own.at[0], load_sem.at[0])
    load_y.start()
    load_x.start()

    barrier = pltpu.get_barrier_semaphore()

    def signal(to):
        pl.semaphore_signal(barrier, inc=1, device_id=to, device_id_type=MESH)

    def receiver(slot):
        holder = served(slot)
        return device(holder["group"] + step(core), holder["blk"] + 3 * step(core))

    signal(along(1))

    @pl.when(jnp.logical_not(first))
    def _():
        signal(across(1))

    @pl.when(jnp.logical_not(blk_end))
    def _():
        signal(along(0))

    @pl.when(jnp.logical_not(blk_end | last))
    def _():
        signal(across(0))

    def each_late_relay(use):
        holder = device(group - step(late), blk - 3 * step(late))
        for j in range(PARTS):
            use(relay_of(late, holder, j), holder)

    @pl.when(edge & low_z)
    def _():
        each_late_relay(lambda to, holder: signal(to))

    signal(served(0))

    @pl.when(hub)
    def _():
        signal(at(0, y, z, core))
        signal(at(3, y, z, core))

    @pl.when(inner & low_z)
    def _():
        signal(receiver(0))

    @pl.when(hub & low_z)
    def _():
        signal(receiver(1))
        signal(receiver(2))

    senders = jnp.where(edge, PARTS + 3, 4) - jnp.where(blk_start, jnp.where(first, 1, 2), 0)
    passing = jnp.where(outer, 1, jnp.where(low_z, 0, jnp.where(hub, 3, 1)))
    pl.semaphore_wait(barrier, senders + passing + jnp.where(edge & jnp.logical_not(low_z), PARTS, 0))

    def go(k, to):
        pl.semaphore_signal(go_sem.at[k], inc=1, device_id=to, device_id_type=MESH)

    @pl.when(edge & jnp.logical_not(low_z))
    def _():
        def tell(to, holder):
            go(slot_of(lax.rem(holder["blk"], 4)), to)

        each_late_relay(tell)

    @pl.when(blk_end)
    def _():
        go(3, along(0))

    @pl.when(blk_end & jnp.logical_not(last))
    def _():
        go(4, across(0))

    load_y.wait()
    load_x.wait()

    def copy(kind, leg, j, source, to):
        k = kind * 12 + leg * 4 + j
        return pltpu.make_async_remote_copy(
            src_ref=source, dst_ref=far.at[kind, leg, rows_of(j)], send_sem=send_sem.at[k], recv_sem=recv_sem.at[k],
            device_id=to, device_id_type=MESH,
        )

    def leg0(kind, j):
        return copy(kind, 0, j, own.at[kind, rows_of(j)], along(kind))

    def leg1(kind, j):
        return copy(kind, 1, j, far.at[kind, 0, rows_of(j)], across(kind))

    def leg2(kind, j):
        back = edge & (late == kind)
        return copy(kind, 2, j, far.at[kind, 1, rows_of(j)], device(group, blk + jnp.where(back, -step(kind), step(kind))))

    def hop(source, target, k_send, k_recv, to):
        return pltpu.make_async_remote_copy(
            src_ref=source, dst_ref=target, send_sem=send_sem.at[k_send], recv_sem=recv_sem.at[k_recv],
            device_id=to, device_id_type=MESH,
        )

    def to_relay(j):
        return hop(own.at[near, rows_of(j)], relay.at[0], near * 12 + 4 + j, 24, at(x, j, z, near))

    def pass_on():
        return hop(relay.at[0], relay.at[slot_of(x)], 24, 24 + slot_of(x), pass_to)

    def from_relay(slot):
        return hop(relay.at[slot], far.at[core, 1, rows_of(y)], 24 + slot, core * 12 + 4 + y, receiver(slot))

    @pl.when(edge)
    def _():
        for j in range(PARTS):
            to_relay(j).start()

    leg0(0, 0).start()

    @pl.when(jnp.logical_not(blk_start))
    def _():
        leg0(1, 0).start()
        leg0(1, 1).start()

    leg0(0, 1).start()

    scale = jnp.exp(jnp.full((1, rows), temp_ref[0], F32))
    shift = bias_ref[0]

    def pair(products):
        logits = scale[:, : products.shape[1]] * products + shift
        small = jnp.exp(-jnp.abs(logits))
        total = 1.0 + small
        log1p = jnp.where(total == 1.0, small, jnp.log(total) * (small / (total - 1.0)))
        weights = jnp.where(logits >= 0, 1.0, small) / total
        return jnp.maximum(logits, 0.0) + log1p, weights * scale[:, : products.shape[1]]

    def held(kind):
        return own_high[kind], own_low[kind]

    def own_part(j, _):
        here = rows_of(j)
        for kind in range(2):
            own_high[kind, here], own_low[kind, here] = split(own[kind, here])
        return 0

    lax.fori_loop(0, PARTS, own_part, 0)

    losses, weights = pair(dot3(held(1), held(0), NT))
    loss_part[0] = losses[:, :128] + losses[:, 128:]
    grad[0] = dot3(split(weights), held(0), NN)
    grad[1] = dot3(split(weights.T), held(1), NN)

    def meet_half(kind, leg, half):
        lines = rows // 2
        other = split(far[kind, leg, half * lines : (half + 1) * lines])
        mine = 1 - kind
        losses, weights = pair(dot3((own_high[mine], own_low[mine]), other, NT))
        loss_part[kind] += losses
        grad[kind] += dot3(split(weights), other, NN)

    def meet(kind, leg):
        def part_of(j, _):
            here = rows_of(j)
            high[here], low[here] = split(far[kind, leg, here])
            return 0

        lax.fori_loop(0, PARTS, part_of, 0)
        other = (high[...], low[...])
        mine = 1 - kind
        losses, weights = pair(dot3((own_high[mine], own_low[mine]), other, NT))
        loss_part[kind] += losses[:, :128] + losses[:, 128:]
        grad[kind] += dot3(split(weights), other, NN)

    loss_part[1] = jnp.zeros_like(loss_part[1])

    def take0(j):
        for kind in range(2):
            leg0(kind, j).wait_recv()

            @pl.when(jnp.logical_not(edge & (near == kind)))
            def _():
                leg1(kind, j).start()

            leg0(kind, j).wait_send()
            if j + 2 < PARTS:
                leg0(kind, j + 2).start()

    def take1(kind, j):
        leg1(kind, j).wait_recv()
        leg2(kind, j).start()

    def take1_ordinary(j):
        @pl.when(edge)
        def _():
            take1(near, j)

        @pl.when(jnp.logical_not(edge))
        def _():
            take1(0, j)
            take1(1, j)

    @pl.when(blk_start)
    def _():
        pl.semaphore_wait(go_sem.at[3], 1)
        leg0(1, 0).start()
        leg0(1, 1).start()

    @pl.when(blk_start & jnp.logical_not(first))
    def _():
        pl.semaphore_wait(go_sem.at[4], 1)

    hop(relay.at[0], relay.at[0], 24, 24, along(0)).wait_recv()

    @pl.when(outer)
    def _():
        pass_on().start()

    @pl.when(inner & jnp.logical_not(low_z))
    def _():
        from_relay(0).start()

    take0(0)

    @pl.when(inner & low_z)
    def _():
        pl.semaphore_wait(go_sem.at[0], 1)
        from_relay(0).start()

    for slot in (1, 2):
        @pl.when(hub & low_z)
        def _():
            pl.semaphore_wait(go_sem.at[slot], 1)

        @pl.when(hub)
        def _():
            hop(relay.at[slot], relay.at[slot], 24 + slot, 24 + slot, along(0)).wait_recv()
            from_relay(slot).start()

    take0(1)

    take1_ordinary(0)
    take0(2)
    take1_ordinary(1)
    take0(3)
    meet(0, 0)
    take1_ordinary(2)
    meet(1, 0)
    take1_ordinary(3)
    meet(near, 1)

    @pl.when(edge)
    def _():
        for j in range(PARTS):
            take1(late, j)

    meet(late, 1)
    write_x = pltpu.make_async_copy(grad.at[0], gx_hbm, out_sem.at[0])
    write_y = pltpu.make_async_copy(grad.at[1], gy_hbm, out_sem.at[1])

    def last_half(kind, half):
        for j in range(half * PARTS // 2, (half + 1) * PARTS // 2):
            leg2(kind, j).wait_recv()
        meet_half(kind, 2, half)

    last_half(near, 0)
    last_half(late, 0)
    last_half(near, 1)

    @pl.when(near == 1)
    def _():
        write_y.start()

    @pl.when(near == 0)
    def _():
        write_x.start()

    last_half(late, 1)

    @pl.when(near == 1)
    def _():
        write_x.start()

    @pl.when(near == 0)
    def _():
        write_y.start()

    loss_ref[...] = lax.dot_general(
        jnp.ones((8, 128), F32), loss_part[0], NT, precision=lax.Precision.HIGHEST, preferred_element_type=F32
    )

    for kind in range(2):
        for j in range(PARTS):
            leg1(kind, j).wait_send()
            leg2(kind, j).wait_send()

    from_relay(0).wait_send()

    @pl.when(hub)
    def _():
        from_relay(1).wait_send()
        from_relay(2).wait_send()

    write_x.wait()
    write_y.wait()


def body(images, held_text, log_temp, bias):
    rows, width = images.shape
    pieces = pltpu.VMEM((2, rows, width), F32)
    halves = pltpu.VMEM((2, rows, width), BF16)
    half = pltpu.VMEM((rows, width), BF16)
    in_hbm = pl.BlockSpec(memory_space=pltpu.HBM)
    scalar = pl.BlockSpec(memory_space=pltpu.SMEM)
    whole = jax.ShapeDtypeStruct((rows, width), F32)
    losses, grad_x, grad_y = pl.pallas_call(
        kernel,
        out_shape=(jax.ShapeDtypeStruct((8, rows), F32), whole, whole),
        in_specs=[scalar, scalar, in_hbm, in_hbm],
        out_specs=(pl.BlockSpec(memory_space=pltpu.VMEM), in_hbm, in_hbm),
        scratch_shapes=[
            pieces, halves, halves,
            pltpu.VMEM((2, 3, rows, width), F32),
            half, half, pieces,
            pltpu.VMEM((3, rows // PARTS, width), F32),
            pltpu.VMEM((2, rows, 128), F32),
            pltpu.SemaphoreType.DMA((2,)),
            pltpu.SemaphoreType.DMA((27,)),
            pltpu.SemaphoreType.DMA((27,)),
            pltpu.SemaphoreType.DMA((2,)),
            pltpu.SemaphoreType.REGULAR((5,)),
        ],
        compiler_params=pltpu.CompilerParams(
            collective_id=0, has_side_effects=True, vmem_limit_bytes=51 * 1024 * 1024
        ),
        name="pair_tiles",
    )(log_temp, bias, images, held_text)
    gain = 1.0 / math.sqrt(4 * rows)
    return losses[0] * (1.0 / (4 * rows)), grad_x * gain, grad_y * gain


def solution(mesh):
    placed = (P(("group", "blk"), None), P(("group", "blk"), None), P(), P())
    return jax.shard_map(
        body,
        mesh=mesh,
        in_specs=placed,
        out_specs=(P(("group", "blk")), P(("group", "blk"), None), P(("group", "blk"), None)),
        check_vma=False,
    )
```
